768 devices in a mesh: ep: 64 (over x, y, z_hi), dp: 12 (over z_lo, core).
Axes of the slice: x: 4, y: 8, z: 12 (z_hi: 2, z_lo: 6; z = z_hi * 6 + z_lo), core: 2. Of those that a mesh axis runs over, the one named last changes fastest.
Arguments:
- out_grad: bfloat16 [1024, 2048], P('ep'), may hold values from -6 to 6
- route_probs: float32 [1024, 8], P('ep'), may hold values from 0.02 to 0.3
- routes: int32 [1024, 8], P('ep'), may hold values from 0 to 127, all different within a row; in each aligned block of 16 rows (0 to 15, 16 to 31, ...) at most 2 rows name the same one
- replica_expert: int32 [64], replicated, may hold values from 0 to 63, as said below
- saved_inputs: bfloat16 [64, 2, 64, 2, 2048], P('ep'), may hold values from -6 to 6
- home_gate_up: bfloat16 [64, 2, 2048, 1536], P('ep', None, None, 'dp'), may hold values from -1 to 1
- home_down: bfloat16 [64, 1536, 2048], P('ep', 'dp'), may hold values from -1 to 1
- replica_gate_up: bfloat16 [64, 2, 2048, 1536], P('ep', None, None, 'dp'), may hold values from -1 to 1, as said below
- replica_down: bfloat16 [64, 1536, 2048], P('ep', 'dp'), may hold values from -1 to 1, as said below
Outputs:
- input_grad: bfloat16 [1024, 2048], P('ep')
- grad_gate_up: bfloat16 [64, 2, 2048, 1536], P('ep', None, None, 'dp')
- grad_down: bfloat16 [64, 1536, 2048], P('ep', 'dp')
The draws below stay inside these ranges and needn't reach their ends.
Inputs may be any that keep to these rules, and one draw needn't show every extreme that they name: `routes`: each token names 8 different slots; slot s lies at index s // 2 of ep as its slot s % 2. Among the tokens of one index of ep no slot is named more than 2 times, a bound that some block reaches. `replica_expert`: entry c is c or c + 1; the last entry is 63. replica_gate_up[c] equals home_gate_up[replica_expert[c]]. replica_down[c] equals home_down[replica_expert[c]].
All inputs are finite; a program needn't handle non-finite values.
Results may differ from the reference program's by a relative error of at most 0.022.
Values may be sent and summed in bfloat16 or wider, within the bound.
No kernel may reach another device: no remote copies, remote signals or barrier semaphores. Data moves between devices by JAX's collectives and lax.ppermute only.
A program may use at most 64 MiB of HBM per device.

```python
import math
import jax
import jax.numpy as jnp
import numpy as np
from jax import lax

D = 2048
FF = 1536
TOPK = 8
T_DEV = 16
EXPERTS = 64
SLOTS = 128
CAP = 2
TOKENS = 1024
N_EP = 64
N_DP = 12


def replica_runs(key):
    key = jax.random.fold_in(key, 11)
    columns = lax.iota(jnp.int32, N_EP)
    step_bits = jax.random.randint(key, (N_EP,), 0, 2)
    return jnp.where(columns == N_EP - 1, columns, columns + step_bits).astype(jnp.int32)


def expert_table(key, salt_value, array_shape, fan_in):
    key = jax.random.fold_in(key, salt_value)
    values = jax.random.normal(key, array_shape, jnp.float32) * fan_in ** (-0.5)
    return jnp.clip(values, -6.0 * fan_in ** (-0.5), 6.0 * fan_in ** (-0.5))


def draw_replica_expert(key, part):
    return replica_runs(key)


def draw_home_gate_up(key, part):
    return expert_table(key, 21, (EXPERTS, 2, D, FF), D).astype(jnp.bfloat16)


def draw_home_down(key, part):
    return expert_table(key, 22, (EXPERTS, FF, D), FF).astype(jnp.bfloat16)


def draw_replica_gate_up(key, part):
    replica_map = replica_runs(key)
    return jnp.take(expert_table(key, 21, (EXPERTS, 2, D, FF), D), replica_map, axis=0).astype(jnp.bfloat16)


def draw_replica_down(key, part):
    replica_map = replica_runs(key)
    return jnp.take(expert_table(key, 22, (EXPERTS, FF, D), FF), replica_map, axis=0).astype(jnp.bfloat16)


def shard_levels(own_key, dims, pieces, least, top_value):
    def one(axis_at, blocks):
        steps = jax.random.uniform(jax.random.fold_in(jax.random.fold_in(own_key, 6), axis_at), (blocks,), jnp.float32, least / len(pieces), top_value / len(pieces))
        return jnp.repeat(jnp.exp(steps), dims[axis_at] // blocks).reshape((-1,) + (1,) * (len(dims) - axis_at - 1))

    factor_of = one(*pieces[0])
    for cut in pieces[1:]:
        factor_of = factor_of * one(*cut)
    return factor_of


def shared_out(key, own, number, rows, count, top, limit, slope):
    ranking = jax.random.permutation(key, count)
    heavy_load, ordinary = load_shares(count, rows * top, limit, slope, True), load_shares(count, rows * top, limit, slope, False)
    places = jnp.arange(count)

    def named(lengths, offset_by):
        used = int((lengths > 0).sum())
        fixed = max(1, used // 4)
        shifted = fixed + (places - fixed + offset_by * (used - fixed)) % max(1, count - fixed)
        return jnp.zeros((count,), jnp.int32).at[ranking[jnp.where(places < fixed, places, shifted)]].set(jnp.asarray(lengths, jnp.int32))

    lengths = jnp.where(number % 4 == 0, named(heavy_load, number // 4), named(ordinary, number - number // 4 - 1))
    mixed = jax.random.permutation(jax.random.fold_in(own, 3), count)
    source_of, sink = mixed[0:count // 2 * 2:2], mixed[1:count // 2 * 2:2]
    margin = jnp.minimum(lengths[source_of] - 1, limit - lengths[sink]) // 2
    margin = jnp.where((source_of == ranking[0]) | (sink == ranking[0]) | (lengths[sink] == 0), 0, jnp.maximum(margin, 0))
    shifted = jax.random.randint(jax.random.fold_in(own, 4), (count // 2,), 0, 1 << 20) % (margin + 1)
    lengths = lengths.at[source_of].add(-shifted).at[sink].add(shifted)
    items = jnp.searchsorted(jnp.cumsum(lengths), jnp.arange(rows * top), side="right").astype(jnp.int32)
    table = items.reshape(top, rows).T
    table = table[jax.random.permutation(jax.random.fold_in(own, 1), rows)]
    offset_by = jax.random.randint(jax.random.fold_in(own, 2), (rows, 1), 0, top)
    return jnp.take_along_axis(table, (jnp.arange(top)[None, :] + offset_by) % top, axis=1)


def load_shares(amount, total, reach, skew, full):
    portions = [(1 << 20) // math.isqrt(rank ** skew) + 1 for rank in range(1, amount + 1)]
    largest = reach if full else min(reach, max(-(-total // amount), total * portions[0] // sum(portions)))
    least = 1 if total - largest >= amount - 1 else 0
    holding, surplus = [largest] + [least] * (amount - 1), total - largest - least * (amount - 1)
    while surplus > 0:
        candidates = [i for i in range(1, amount) if holding[i] < largest] or [i for i in range(1, amount) if holding[i] < reach]
        mass, left = sum([portions[i] for i in candidates]), surplus
        for i in candidates:
            addition = min(reach - holding[i], max(1, left * portions[i] // mass), surplus)
            holding[i] = holding[i] + addition
            surplus = surplus - addition
    return np.array(holding)


def bell_draw(own_key, extent, scale, reach, cuts=(), kind=jnp.bfloat16):
    array = scale * jax.random.normal(own_key, extent, jnp.float32)
    if cuts:
        array = array * shard_levels(own_key, extent, cuts, -0.22, 0.18)
    return jnp.clip(array, -reach, reach).astype(kind)


def setup_inputs(seed: int = 0) -> dict:
    arg_keys = jax.random.split(jax.random.key(seed), 10)
    out_grad = bell_draw(arg_keys[0], (TOKENS, D), 1.0, 6.0, ((0, 64),))
    route_probs = jnp.clip(0.02 + 0.28 * jax.random.uniform(arg_keys[1], (TOKENS, TOPK), jnp.float32) ** shard_levels(arg_keys[1], (TOKENS, TOPK), ((0, 64),), -0.2, 0.2), 0.02, 0.3)
    routes_keys = jax.random.split(jax.random.fold_in(arg_keys[2], 1), TOKENS // T_DEV)
    routes_turns = jax.random.permutation(jax.random.fold_in(arg_keys[2], 3), TOKENS // T_DEV)
    routes = jax.vmap(lambda own, number: shared_out(jax.random.fold_in(arg_keys[2], 2), own, number, T_DEV, SLOTS, TOPK, CAP, 2))(routes_keys, routes_turns).reshape((TOKENS, TOPK))
    replica_expert = draw_replica_expert(jax.random.fold_in(arg_keys[9], 71), 0)
    saved_inputs = bell_draw(arg_keys[4], (EXPERTS, 2, EXPERTS, CAP, D), 1.0, 6.0, ((0, 64),))
    home_gate_up = draw_home_gate_up(jax.random.fold_in(arg_keys[9], 71), 0)
    home_down = draw_home_down(jax.random.fold_in(arg_keys[9], 71), 0)
    replica_gate_up = draw_replica_gate_up(jax.random.fold_in(arg_keys[9], 71), 0)
    replica_down = draw_replica_down(jax.random.fold_in(arg_keys[9], 71), 0)
    return dict(out_grad=out_grad, route_probs=route_probs, routes=routes, replica_expert=replica_expert, saved_inputs=saved_inputs, home_gate_up=home_gate_up, home_down=home_down, replica_gate_up=replica_gate_up, replica_down=replica_down)


def slot_terms(inputs, block_grad, gate_up, down_weight):
    gate_pre = jnp.dot(inputs, gate_up[0], preferred_element_type=jnp.float32)
    up_pre = jnp.dot(inputs, gate_up[1], preferred_element_type=jnp.float32)
    sigmoid_gate = jax.nn.sigmoid(gate_pre)
    active = gate_pre * sigmoid_gate
    hidden = (active * up_pre).astype(jnp.bfloat16)
    hidden_grad = jnp.dot(block_grad, down_weight.T, preferred_element_type=jnp.float32)
    up_grad = (hidden_grad * active).astype(jnp.bfloat16)
    gate_grad = (hidden_grad * up_pre * sigmoid_gate * (1.0 + gate_pre * (1.0 - sigmoid_gate))).astype(jnp.bfloat16)
    weight_gate = jnp.dot(inputs.T, gate_grad, preferred_element_type=jnp.float32)
    weight_up = jnp.dot(inputs.T, up_grad, preferred_element_type=jnp.float32)
    weight_down = jnp.dot(hidden.T, block_grad, preferred_element_type=jnp.float32)
    row_count = inputs.shape[0]
    gate_blocks = gate_grad.astype(jnp.float32).reshape(row_count, N_DP, FF // N_DP)
    up_blocks = up_grad.astype(jnp.float32).reshape(row_count, N_DP, FF // N_DP)
    gate_columns = gate_up[0].astype(jnp.float32).reshape(D, N_DP, FF // N_DP)
    up_columns = gate_up[1].astype(jnp.float32).reshape(D, N_DP, FF // N_DP)
    block_sums = jnp.einsum("rnf,dnf->nrd", gate_blocks, gate_columns)
    block_sums = block_sums + jnp.einsum("rnf,dnf->nrd", up_blocks, up_columns)
    rounded = lax.optimization_barrier(block_sums.astype(jnp.bfloat16)).astype(jnp.float32)
    row_grad = jnp.sum(rounded, axis=0).astype(jnp.bfloat16)
    return row_grad, (weight_gate, weight_up, weight_down)


def reference(out_grad, route_probs, routes, replica_expert, saved_inputs, home_gate_up, home_down, replica_gate_up, replica_down):
    route_count = T_DEV * TOPK
    routed_grad = (route_probs[:, :, None] * out_grad[:, None, :].astype(jnp.float32)).astype(jnp.bfloat16)
    slot_rows = routes.reshape(N_EP, route_count).astype(jnp.int32)
    slot_ids = jnp.arange(2 * N_EP, dtype=jnp.int32)
    matches = (slot_rows[:, :, None] == slot_ids[None, None, :]).astype(jnp.int32)
    position = jnp.sum((jnp.cumsum(matches, axis=1) - matches) * matches, axis=2).astype(jnp.int32)
    sources = jnp.broadcast_to(jnp.arange(N_EP, dtype=jnp.int32)[:, None], slot_rows.shape)
    blocks = jnp.zeros((2 * N_EP, N_EP, CAP, D), jnp.bfloat16)
    blocks = blocks.at[slot_rows, sources, position].set(routed_grad.reshape(N_EP, route_count, D))

    def per_holder(totals, column):
        inputs = saved_inputs[column]
        grad_blocks = lax.dynamic_slice_in_dim(blocks, 2 * column, 2, 0)
        home_rows, home_parts = slot_terms(inputs[0].reshape(-1, D), grad_blocks[0].reshape(-1, D), home_gate_up[column], home_down[column])
        spare_rows, spare_parts = slot_terms(inputs[1].reshape(-1, D), grad_blocks[1].reshape(-1, D), replica_gate_up[column], replica_down[column])
        expert_spare = replica_expert[column]
        totals = tuple(total_part.at[column].add(home_part).at[expert_spare].add(spare_part) for total_part, home_part, spare_part in zip(totals, home_parts, spare_parts))
        return totals, jnp.stack([home_rows, spare_rows])

    start_totals = (jnp.zeros((EXPERTS, D, FF), jnp.float32), jnp.zeros((EXPERTS, D, FF), jnp.float32), jnp.zeros((EXPERTS, FF, D), jnp.float32))
    totals, all_rows = lax.scan(per_holder, start_totals, jnp.arange(N_EP, dtype=jnp.int32))
    all_rows = all_rows.reshape(N_EP, 2, N_EP, CAP, D)
    picked = all_rows[slot_rows // 2, slot_rows % 2, sources, position]
    input_grad = jnp.sum(picked.astype(jnp.float32).reshape(TOKENS, TOPK, D), axis=1).astype(jnp.bfloat16)
    grad_gate_up = jnp.stack([totals[0], totals[1]], axis=1).astype(jnp.bfloat16)
    grad_down = totals[2].astype(jnp.bfloat16)
    return (input_grad, grad_gate_up, grad_down)
```

```python
import jax
import jax.numpy as jnp
from jax import lax
from jax.sharding import PartitionSpec as P

BF = jnp.bfloat16
F32 = jnp.float32
COLS = (((1,), (1,)), ((), ()))
ROWS = (((0,), (0,)), ((), ()))


def along_dp(array, to):
    pairs = [(2 * z + c, 2 * to(z)[0] + (c ^ to(z)[1])) for z in range(6) for c in range(2)]
    return lax.ppermute(array, "dp", pairs)


def swap_cores(array):
    return along_dp(array, lambda z: (z, 1))


def to_next(array):
    length = lax.axis_size("ep")
    return lax.ppermute(array, "ep", [(i, i + 1) for i in range(length - 1)])


def exchange(array):
    return lax.all_to_all(array, "ep", split_axis=0, concat_axis=0, tiled=True)


def joined(own, other, core):
    first = jnp.where(core == 0, own, other)
    second = jnp.where(core == 0, other, own)
    return jnp.concatenate([first, second], axis=-1)


def act(x, gate_up):
    gate = jnp.dot(x, gate_up[0], preferred_element_type=F32)
    up = jnp.dot(x, gate_up[1], preferred_element_type=F32)
    sig = jax.nn.sigmoid(gate)
    active = gate * sig
    hidden = (active * up).astype(BF)
    slope = up * sig * (1.0 + gate * (1.0 - sig))
    return active, slope, hidden


def hidden_grads(block, down, active, slope):
    hg = lax.dot_general(block, down, COLS, preferred_element_type=F32)
    return (hg * slope).astype(BF), (hg * active).astype(BF)


def on_device(
    out_grad,
    route_probs,
    routes,
    replica_expert,
    saved_inputs,
    home_gate_up,
    home_down,
    replica_gate_up,
    replica_down,
):
    n_ep = lax.axis_size("ep")
    tokens, top = routes.shape
    width = out_grad.shape[1]
    half = width // 2
    cap = saved_inputs.shape[3]
    rows = n_ep * cap
    column = lax.axis_index("ep")
    core = lax.axis_index("dp") % 2

    spare_half = lax.dynamic_slice_in_dim(saved_inputs[0, 1], core * half, half, 2)
    prior_x_own = to_next(spare_half)

    slot_ids = lax.iota(jnp.int32, 2 * n_ep)
    names = routes[:, :, None] == slot_ids[None, None, :]
    named = jnp.any(names, axis=1)
    prob_ts = jnp.sum(jnp.where(names, route_probs[:, :, None], 0.0), axis=1)
    earlier = jnp.cumsum(named.astype(jnp.int32), axis=0) - named.astype(jnp.int32)
    place = jnp.stack([named & (earlier == p) for p in range(cap)])
    row_prob = jnp.sum(jnp.where(place, prob_ts[None], 0.0), axis=1)
    table = place.astype(BF).transpose(2, 0, 1).reshape(n_ep * 2 * cap, tokens)
    row_prob = row_prob.T.reshape(n_ep * 2 * cap, 1)
    out_half = lax.dynamic_slice_in_dim(out_grad, core * half, half, 1)
    outgoing = (jnp.dot(table, out_half, preferred_element_type=F32) * row_prob).astype(BF)
    incoming = exchange(outgoing.reshape(n_ep, 16, half // 4))

    held = saved_inputs.reshape(2, rows, width)
    home_act = act(held[0], home_gate_up[0])
    spare_act = act(held[1], replica_gate_up[0])
    prior_x = joined(prior_x_own, swap_cores(prior_x_own), core).reshape(rows, width)
    prior_act = act(prior_x, home_gate_up[0])

    other_in = swap_cores(incoming)
    block = joined(
        incoming.reshape(n_ep, 2 * cap, half), other_in.reshape(n_ep, 2 * cap, half), core
    )
    block = block.reshape(n_ep, 2, cap, width)
    block_home = block[:, 0].reshape(rows, width)
    block_spare = block[:, 1].reshape(rows, width)
    gg_home, ug_home = hidden_grads(block_home, home_down[0], home_act[0], home_act[1])
    gg_spare, ug_spare = hidden_grads(block_spare, replica_down[0], spare_act[0], spare_act[1])

    def back(start):
        parts = []
        for gg, ug, w in ((gg_home, ug_home, home_gate_up[0]), (gg_spare, ug_spare, replica_gate_up[0])):
            wg = lax.dynamic_slice_in_dim(w, start, half, 1)
            part = lax.dot_general(gg, wg[0], COLS, preferred_element_type=F32)
            parts.append(part + lax.dot_general(ug, wg[1], COLS, preferred_element_type=F32))
        return jnp.stack([p.reshape(n_ep, cap, half) for p in parts], axis=1)

    sent = back((1 - core) * half).astype(BF).reshape(n_ep, 16, half // 4)
    kept = back(core * half)
    pair_sum = kept.reshape(n_ep, 16, half // 4) + swap_cores(sent).astype(F32)
    returned = exchange(pair_sum.astype(BF))

    back_table = table.reshape(n_ep * 2 * cap, tokens)
    mine = lax.dot_general(
        back_table, returned.reshape(n_ep * 2 * cap, half), ROWS, preferred_element_type=F32
    )
    total = mine + along_dp(mine.astype(BF), lambda z: (z ^ 1, 0)).astype(F32)
    low = total.astype(BF)
    one = along_dp(low, lambda z: ((z + 2) % 6, 0))
    two = along_dp(low, lambda z: ((z + 4) % 6, 0))
    total = (total + one.astype(F32) + two.astype(F32)).astype(BF)
    input_grad = joined(total, swap_cores(total), core)

    prior_own = to_next(incoming.reshape(n_ep, 2, 8, half // 4)[:, 1])
    prior_block = joined(
        prior_own.reshape(n_ep, cap, half), swap_cores(prior_own).reshape(n_ep, cap, half), core
    ).reshape(rows, width)
    gg_prior, ug_prior = hidden_grads(prior_block, home_down[0], prior_act[0], prior_act[1])

    prior_entry = replica_expert[jnp.maximum(column - 1, 0)]
    keeps_own = replica_expert[column] == column
    takes_prior = (column > 0) & (prior_entry == column)

    def only(array, keep):
        return jnp.where(keep, array, jnp.zeros_like(array))

    all_x = jnp.concatenate([held[0], held[1], only(prior_x, takes_prior)])
    all_block = jnp.concatenate([block_home, block_spare, only(prior_block, takes_prior)])

    def stacked(a, b, c):
        return jnp.concatenate([a, only(b, keeps_own), only(c, takes_prior)])

    gate = lax.dot_general(
        all_x, stacked(gg_home, gg_spare, gg_prior), ROWS, preferred_element_type=F32
    )
    up = lax.dot_general(
        all_x, stacked(ug_home, ug_spare, ug_prior), ROWS, preferred_element_type=F32
    )
    down = lax.dot_general(
        stacked(home_act[2], spare_act[2], prior_act[2]), all_block, ROWS, preferred_element_type=F32
    )
    grad_gate_up = jnp.stack([gate, up])[None].astype(BF)
    return (input_grad, grad_gate_up, down[None].astype(BF))


def solution(mesh):
    placed = (
        P("ep", None),
        P("ep", None),
        P("ep", None),
        P(),
        P("ep", None, None, None, None),
        P("ep", None, None, "dp"),
        P("ep", "dp", None),
        P("ep", None, None, "dp"),
        P("ep", "dp", None),
    )
    return jax.shard_map(
        on_device,
        mesh=mesh,
        in_specs=placed,
        out_specs=(P("ep", None), P("ep", None, None, "dp"), P("ep", "dp", None)),
        check_vma=False,
    )
```

```python
import jax
import jax.numpy as jnp
from jax import lax
from jax.experimental import pallas as pl
from jax.experimental.pallas import tpu as pltpu
from jax.sharding import PartitionSpec as P

BF = jnp.bfloat16
F32 = jnp.float32
NT = (((1,), (1,)), ((), ()))
TN = (((0,), (0,)), ((), ()))
GROUPS = 8
VMEM = pl.BlockSpec(memory_space=pltpu.VMEM)
ANY = pl.BlockSpec(memory_space=pl.ANY)
SMEM = pl.BlockSpec(memory_space=pltpu.SMEM)


def along_dp(array, to):
    pairs = [(2 * z + c, 2 * to(z)[0] + (c ^ to(z)[1])) for z in range(6) for c in range(2)]
    return lax.ppermute(array, "dp", pairs)


def swap_cores(array):
    return along_dp(array, lambda z: (z, 1))


def mirrored(e, dp):
    return 12 * e + (dp if e % 2 == 0 else 10 - dp + 2 * (dp % 2))


def to_next(array):
    length = lax.axis_size("ep")
    pairs = [
        (mirrored(e, dp), mirrored(e + 1, dp)) for e in range(length - 1) for dp in range(12)
    ]
    return lax.ppermute(array, ("ep", "dp"), pairs)


def exchange(array):
    length = lax.axis_size("ep")
    groups = [[mirrored(e, dp) for e in range(length)] for dp in range(12)]
    array = array.reshape(length, -1, 256)
    array = lax.all_to_all(
        array, ("ep", "dp"), split_axis=0, concat_axis=0, axis_index_groups=groups, tiled=True
    )
    return array.reshape(-1, 256)


def dot(a, b, dims=(((1,), (0,)), ((), ()))):
    return lax.dot_general(a, b, dims, preferred_element_type=F32)


def half_at(core):
    return pl.ds(pl.multiple_of(core * 1024, 1024), 1024)


def by_slot():
    row = lax.broadcasted_iota(jnp.int32, (128, 128), 0)
    col = lax.broadcasted_iota(jnp.int32, (128, 128), 1)
    return (col == 16 * (row % 8) + 2 * (row // 16) + row // 8 % 2).astype(F32).astype(BF)


def by_source(kinds):
    row = lax.broadcasted_iota(jnp.int32, (64 * kinds, 64 * kinds), 0)
    col = lax.broadcasted_iota(jnp.int32, (64 * kinds, 64 * kinds), 1)
    want = 8 * kinds * (row // 2 % 8) + 8 * (row // 64) + 4 * (row % 2) + row // 16 % 4
    return (col == want).astype(F32).astype(BF)


def by_prior():
    row = lax.broadcasted_iota(jnp.int32, (128, 128), 0)
    col = lax.broadcasted_iota(jnp.int32, (128, 128), 1)
    return (col == 16 * (row % 8) + row // 8).astype(F32).astype(BF)


def slots():
    return lax.broadcasted_iota(jnp.int32, (128, 16), 0)


def places_of(slot, routes):
    named = jnp.zeros(slot.shape, F32)
    for k in range(8):
        named = named + jnp.where(slot == routes[k : k + 1, :], 1.0, 0.0)
    before = lax.broadcasted_iota(jnp.int32, (16, 16), 0) < lax.broadcasted_iota(
        jnp.int32, (16, 16), 1
    )
    earlier = dot(named.astype(BF), before.astype(F32).astype(BF))
    return [jnp.where(earlier == p, named, 0.0) for p in range(2)]


def routed(slot, routes, probs, half):
    prob = jnp.zeros(slot.shape, F32)
    for k in range(8):
        prob = prob + jnp.where(slot == routes[k : k + 1, :], probs[k : k + 1, :], 0.0)
    places = places_of(slot, routes)
    rows = []
    for place in places:
        row_prob = jnp.sum(place * prob, axis=1, keepdims=True)
        rows.append((dot(place.astype(BF), half) * row_prob).astype(BF))
    return places, rows


def blocks_of(rows, g):
    parts = [
        rows[p][16 * g : 16 * g + 16, 256 * f : 256 * f + 256] for p in range(2) for f in range(4)
    ]
    return jnp.concatenate(parts)


def prep_kernel(routes, probs, out_grad, outgoing):
    half = out_grad[:, half_at(lax.axis_index("dp") % 2)]
    table = by_slot()
    _, rows = routed(slots(), routes, probs, half)
    prior = 2 * lax.broadcasted_iota(jnp.int32, (64, 16), 0) - 1
    _, prior_rows = routed(prior, routes, probs, half)
    prior_table = by_prior()
    for g in range(4):
        held = [dot(table, blocks_of(rows, 2 * g + h)).astype(BF) for h in range(2)]
        extra = dot(prior_table, blocks_of(prior_rows, g)).astype(BF)
        for h in range(2):
            for c in range(8):
                at = 24 * (16 * g + 8 * h + c)
                outgoing[at : at + 16, :] = held[h][16 * c : 16 * c + 16, :]
                outgoing[at + 16 : at + 24, :] = extra[64 * h + 8 * c : 64 * h + 8 * c + 8, :]


def act(x, w_gate, w_up):
    gate = dot(x, w_gate)
    up = dot(x, w_up)
    sig = jax.nn.sigmoid(gate)
    active = gate * sig
    slope = up * sig * (1.0 + gate * (1.0 - sig))
    return active, slope, (active * up).astype(BF)


def act_kernel(x, home_gu, spare_gu, routes, active, slope, hidden, place_out):
    for p, place in enumerate(places_of(slots(), routes)):
        place_out[128 * p : 128 * p + 128, :] = place.astype(BF)
    for j, w in enumerate((home_gu, spare_gu)):
        a, s, h = act(x[128 * j : 128 * j + 128, :], w[0], w[1])
        active[128 * j : 128 * j + 128, :] = a
        slope[128 * j : 128 * j + 128, :] = s
        hidden[128 * j : 128 * j + 128, :] = h


def rows_kernel(
    own_in,
    other_in,
    active_in,
    slope_in,
    home_d,
    spare_d,
    home_gu,
    spare_gu,
    sent_out,
    kept_out,
    grads_out,
    block_out,
    got,
    active,
    slope,
    w_d,
    w_gu,
    block,
    sent,
    kept,
    grads,
    sems,
    out_sems,
):
    core = lax.axis_index("dp") % 2
    here, there = half_at(core), half_at(1 - core)
    pairs = [
        (own_in, got.at[0]),
        (other_in, got.at[1]),
        (home_d, w_d.at[0]),
        (slope_in, slope),
        (active_in, active),
        (home_gu, w_gu.at[0]),
        (spare_d, w_d.at[1]),
        (spare_gu, w_gu.at[1]),
    ]
    loads = [pltpu.make_async_copy(a, b, sems.at[i]) for i, (a, b) in enumerate(pairs)]
    for load in loads:
        load.start()
    table = by_source(3)
    for i, at in enumerate((here, there)):
        loads[i].wait()
        for g in range(GROUPS):
            rows = dot(table, got[i, 192 * g : 192 * g + 192, :]).astype(BF)
            for j in range(3):
                parts = [rows[64 * j + 16 * f : 64 * j + 16 * f + 16, :] for f in range(4)]
                block[128 * j + 16 * g : 128 * j + 16 * g + 16, at] = jnp.concatenate(parts, axis=1)
    stores = [pltpu.make_async_copy(block, block_out, out_sems.at[0])]
    stores[0].start()
    for j in range(2):
        mine = pl.ds(128 * j, 128)
        for i in ((2, 3, 4) if j == 0 else (6,)):
            loads[i].wait()
        hidden_grad = dot(block[mine, :], w_d[j], NT)
        both = jnp.concatenate(
            [(hidden_grad * slope[mine, :]).astype(BF), (hidden_grad * active[mine, :]).astype(BF)],
            axis=1,
        )
        grads[mine, :] = both
        loads[5 if j == 0 else 7].wait()
        weights = jnp.concatenate([w_gu[j, 0, here, :], w_gu[j, 1, here, :]], axis=1)
        kept[mine, :] = dot(both, weights, NT)
        weights = jnp.concatenate([w_gu[j, 0, there, :], w_gu[j, 1, there, :]], axis=1)
        sent[mine, :] = dot(both, weights, NT).astype(BF)
        for i, (a, b) in enumerate(((kept, kept_out), (sent, sent_out), (grads, grads_out))):
            store = pltpu.make_async_copy(a.at[mine], b.at[mine], out_sems.at[1 + 3 * j + i])
            store.start()
            stores.append(store)
    for store in stores:
        store.wait()


def pair_kernel(kept, got, outgoing):
    table = by_source(2)
    for g in range(GROUPS):
        parts = []
        for j in range(2):
            at = slice(128 * j + 16 * g, 128 * j + 16 * g + 16)
            total = (kept[at, :] + got[at, :].astype(F32)).astype(BF)
            parts += [total[:, 256 * f : 256 * f + 256] for f in range(4)]
        outgoing[128 * g : 128 * g + 128, :] = dot(table, jnp.concatenate(parts), TN).astype(BF)


def combine_kernel(returned, place, mine, low, rows):
    table = by_slot()
    for g in range(GROUPS):
        back = dot(table, returned[128 * g : 128 * g + 128, :], TN).astype(BF)
        for p in range(2):
            rows[128 * p + 16 * g : 128 * p + 16 * g + 16, :] = jnp.concatenate(
                [back[16 * (4 * p + f) : 16 * (4 * p + f) + 16, :] for f in range(4)], axis=1
            )
    total = dot(place[...], rows[...], TN)
    mine[...] = total
    low[...] = total.astype(BF)


def weights_kernel(
    experts,
    x,
    x_own,
    x_other,
    block,
    grads,
    hidden,
    home_gu,
    home_d,
    grad_gu,
    grad_d,
    x_prior,
):
    core = lax.axis_index("dp") % 2
    x_prior[pl.ds(pl.multiple_of(64 * core, 64), 64), :] = x_own[...]
    x_prior[pl.ds(pl.multiple_of(64 - 64 * core, 64), 64), :] = x_other[...]
    column = lax.axis_index("ep")
    keeps_own = experts[column] == column
    takes_prior = (column > 0) & (experts[jnp.maximum(column - 1, 0)] == column)
    active, slope, hidden_prior = act(x_prior[...], home_gu[0], home_gu[1])
    hidden_grad = dot(block[256:384, :], home_d[...], NT)
    grads_prior = jnp.concatenate(
        [(hidden_grad * slope).astype(BF), (hidden_grad * active).astype(BF)], axis=1
    )

    def only(keep, array):
        return jnp.where(keep, array, jnp.zeros_like(array))

    grads_spare = only(keeps_own, grads[128:256, :])
    grads_prior = only(takes_prior, grads_prior)
    hidden_spare = only(keeps_own, hidden[128:256, :])
    hidden_prior = only(takes_prior, hidden_prior)
    all_grads = jnp.concatenate([grads[0:128, :], grads_spare, grads_prior])
    all_hidden = jnp.concatenate([hidden[0:128, :], hidden_spare, hidden_prior])
    for i in range(8):
        at = slice(256 * i, 256 * i + 256)
        rows = jnp.concatenate([x[:, at], x_prior[:, at]])
        total = dot(rows, all_grads, TN).astype(BF)
        grad_gu[0, at, :] = total[:, :128]
        grad_gu[1, at, :] = total[:, 128:]
        grad_d[:, at] = dot(all_hidden, block[:, at], TN).astype(BF)


def finish_kernel(own, other, result):
    core = lax.axis_index("dp") % 2
    result[:, half_at(core)] = own[...]
    result[:, half_at(1 - core)] = other[...]


def shape(dims, kind=BF):
    return jax.ShapeDtypeStruct(dims, kind)


def call(kernel, outs, flops, nbytes, specs, scratch=(), into=None, vmem=60):
    return pl.pallas_call(
        kernel,
        out_shape=outs,
        in_specs=specs,
        out_specs=jax.tree.map(lambda _: VMEM, outs) if into is None else into,
        scratch_shapes=scratch,
        cost_estimate=pl.CostEstimate(flops=flops, bytes_accessed=nbytes, transcendentals=0),
        compiler_params=pltpu.CompilerParams(vmem_limit_bytes=vmem << 20),
    )


def on_device(
    out_grad,
    route_probs,
    routes,
    replica_expert,
    saved_inputs,
    home_gate_up,
    home_down,
    replica_gate_up,
    replica_down,
):
    home_gu, home_d = home_gate_up[0], home_down[0]
    spare_gu, spare_d = replica_gate_up[0], replica_down[0]

    core = lax.axis_index("dp") % 2
    x_part = lax.dynamic_slice_in_dim(saved_inputs[0, 1], core * 32, 32, 0)
    x_part, routes, route_probs = lax.optimization_barrier((x_part, routes, route_probs))
    x_part = to_next(x_part)

    outgoing = call(prep_kernel, shape((1536, 256)), 10**6, 10**6, [VMEM] * 3)(
        routes.T, route_probs.T, out_grad
    )
    incoming = exchange(outgoing)

    saved, _ = lax.optimization_barrier((saved_inputs, outgoing))
    x = saved.reshape(256, 2048)
    active, slope, hidden, place = call(
        act_kernel,
        (
            shape((256, 128), F32),
            shape((256, 128), F32),
            shape((256, 128)),
            shape((256, 16)),
        ),
        10**11,
        4 * 10**6,
        [VMEM] * 4,
    )(x, home_gu, spare_gu, routes.T)
    incoming, active, x_part = lax.optimization_barrier((incoming, active, x_part))

    other = swap_cores(incoming)
    sent, kept, grads, block = call(
        rows_kernel,
        (
            shape((256, 1024)),
            shape((256, 1024), F32),
            shape((256, 256)),
            shape((384, 2048)),
        ),
        10**9,
        8 * 10**6,
        [ANY] * 8,
        [
            pltpu.VMEM((2, 1536, 256), BF),
            pltpu.VMEM((256, 128), F32),
            pltpu.VMEM((256, 128), F32),
            pltpu.VMEM((2, 128, 2048), BF),
            pltpu.VMEM((2, 2, 2048, 128), BF),
            pltpu.VMEM((384, 2048), BF),
            pltpu.VMEM((256, 1024), BF),
            pltpu.VMEM((256, 1024), F32),
            pltpu.VMEM((256, 256), BF),
            pltpu.SemaphoreType.DMA((8,)),
            pltpu.SemaphoreType.DMA((7,)),
        ],
        (ANY, ANY, ANY, ANY),
    )(incoming, other, active, slope, home_d, spare_d, home_gu, spare_gu)
    got = swap_cores(sent)
    pair = call(pair_kernel, shape((1024, 256)), 10**8, 2 * 10**6, [VMEM] * 2, vmem=28)(kept, got)
    returned = exchange(pair)

    x_part, _ = lax.optimization_barrier((x_part, pair))
    grad_gu, grad_d = call(
        weights_kernel,
        (shape((2, 2048, 128)), shape((128, 2048))),
        10**8,
        10**6,
        [SMEM] + [VMEM] * 8,
        [pltpu.VMEM((128, 2048), BF)],
    )(
        replica_expert,
        x,
        x_part.reshape(64, 2048),
        swap_cores(x_part).reshape(64, 2048),
        block,
        grads,
        hidden,
        home_gu,
        home_d,
    )
    returned, grad_gu = lax.optimization_barrier((returned, grad_gu))

    mine, low = call(
        combine_kernel,
        (shape((16, 1024), F32), shape((16, 1024))),
        10**8,
        10**6,
        [VMEM] * 2,
        [pltpu.VMEM((256, 1024), BF)],
        vmem=28,
    )(returned, place)
    total = mine + along_dp(low, lambda z: (z ^ 1, 0)).astype(F32)
    low = total.astype(BF)
    one = along_dp(low, lambda z: ((z + 2) % 6, 0))
    two = along_dp(low, lambda z: ((z + 4) % 6, 0))
    total = (total + one.astype(F32) + two.astype(F32)).astype(BF)
    input_grad = call(finish_kernel, shape((16, 2048)), 10**3, 10**5, [VMEM] * 2, vmem=28)(
        total, swap_cores(total)
    )
    return (input_grad, grad_gu[None], grad_d[None])


def solution(mesh):
    placed = (
        P("ep", None),
        P("ep", None),
        P("ep", None),
        P(),
        P("ep", None, None, None, None),
        P("ep", None, None, "dp"),
        P("ep", "dp", None),
        P("ep", None, None, "dp"),
        P("ep", "dp", None),
    )
    return jax.shard_map(
        on_device,
        mesh=mesh,
        in_specs=placed,
        out_specs=(P("ep", None), P("ep", None, None, "dp"), P("ep", "dp", None)),
        check_vma=False,
    )
```

```python
import jax
import jax.numpy as jnp
from jax import lax
from jax.experimental import pallas as pl
from jax.experimental.pallas import tpu as pltpu
from jax.sharding import PartitionSpec as P

BF = jnp.bfloat16
F32 = jnp.float32
NT = (((1,), (1,)), ((), ()))
TN = (((0,), (0,)), ((), ()))
GROUPS = 8
VMEM = pl.BlockSpec(memory_space=pltpu.VMEM)
ANY = pl.BlockSpec(memory_space=pl.ANY)
SMEM = pl.BlockSpec(memory_space=pltpu.SMEM)


def along_dp(array, to):
    pairs = [(2 * z + c, 2 * to(z)[0] + (c ^ to(z)[1])) for z in range(6) for c in range(2)]
    return lax.ppermute(array, "dp", pairs)


def swap_cores(array):
    return along_dp(array, lambda z: (z, 1))


def mirrored(e, dp):
    return 12 * e + (dp if e % 2 == 0 else 10 - dp + 2 * (dp % 2))


def to_next(array):
    length = lax.axis_size("ep")
    pairs = [
        (mirrored(e, dp), mirrored(e + 1, dp)) for e in range(length - 1) for dp in range(12)
    ]
    return lax.ppermute(array, ("ep", "dp"), pairs)


def exchange(array):
    length = lax.axis_size("ep")
    groups = [[mirrored(e, dp) for e in range(length)] for dp in range(12)]
    array = array.reshape(length, -1, 256)
    array = lax.all_to_all(
        array, ("ep", "dp"), split_axis=0, concat_axis=0, axis_index_groups=groups, tiled=True
    )
    return array.reshape(-1, 256)


def dot(a, b, dims=(((1,), (0,)), ((), ()))):
    return lax.dot_general(a, b, dims, preferred_element_type=F32)


def half_at(core):
    return pl.ds(pl.multiple_of(core * 1024, 1024), 1024)


def by_slot():
    row = lax.broadcasted_iota(jnp.int32, (128, 128), 0)
    col = lax.broadcasted_iota(jnp.int32, (128, 128), 1)
    return (col == 16 * (row % 8) + 2 * (row // 16) + row // 8 % 2).astype(F32).astype(BF)


def by_source(kinds):
    row = lax.broadcasted_iota(jnp.int32, (64 * kinds, 64 * kinds), 0)
    col = lax.broadcasted_iota(jnp.int32, (64 * kinds, 64 * kinds), 1)
    want = 8 * kinds * (row // 2 % 8) + 8 * (row // 64) + 4 * (row % 2) + row // 16 % 4
    return (col == want).astype(F32).astype(BF)


def by_prior():
    row = lax.broadcasted_iota(jnp.int32, (128, 128), 0)
    col = lax.broadcasted_iota(jnp.int32, (128, 128), 1)
    return (col == 16 * (row % 8) + row // 8).astype(F32).astype(BF)


def slots():
    return lax.broadcasted_iota(jnp.int32, (128, 16), 0)


def places_of(slot, routes):
    named = jnp.zeros(slot.shape, F32)
    for k in range(8):
        named = named + jnp.where(slot == routes[k : k + 1, :], 1.0, 0.0)
    before = lax.broadcasted_iota(jnp.int32, (16, 16), 0) < lax.broadcasted_iota(
        jnp.int32, (16, 16), 1
    )
    earlier = dot(named.astype(BF), before.astype(F32).astype(BF))
    return [jnp.where(earlier == p, named, 0.0) for p in range(2)]


def routed(slot, routes, probs, half):
    prob = jnp.zeros(slot.shape, F32)
    for k in range(8):
        prob = prob + jnp.where(slot == routes[k : k + 1, :], probs[k : k + 1, :], 0.0)
    places = places_of(slot, routes)
    rows = []
    for place in places:
        row_prob = jnp.sum(place * prob, axis=1, keepdims=True)
        rows.append((dot(place.astype(BF), half) * row_prob).astype(BF))
    return places, rows


def blocks_of(rows, g):
    parts = [
        rows[p][16 * g : 16 * g + 16, 256 * f : 256 * f + 256] for p in range(2) for f in range(4)
    ]
    return jnp.concatenate(parts)


def prep_kernel(routes, probs, out_grad, outgoing_out, outgoing, sems):
    stores = []
    half = out_grad[:, half_at(lax.axis_index("dp") % 2)]
    table = by_slot()
    _, rows = routed(slots(), routes, probs, half)
    prior = 2 * lax.broadcasted_iota(jnp.int32, (64, 16), 0) - 1
    _, prior_rows = routed(prior, routes, probs, half)
    prior_table = by_prior()
    for g in range(4):
        held = [dot(table, blocks_of(rows, 2 * g + h)).astype(BF) for h in range(2)]
        extra = dot(prior_table, blocks_of(prior_rows, g)).astype(BF)
        for h in range(2):
            for c in range(8):
                at = 24 * (16 * g + 8 * h + c)
                outgoing[at : at + 16, :] = held[h][16 * c : 16 * c + 16, :]
                outgoing[at + 16 : at + 24, :] = extra[64 * h + 8 * c : 64 * h + 8 * c + 8, :]
        done = pl.ds(384 * g, 384)
        stores.append(
            pltpu.make_async_copy(outgoing.at[done], outgoing_out.at[done], sems.at[g])
        )
        stores[g].start()
    for store in stores:
        store.wait()


def act(x, w_gate, w_up):
    gate = dot(x, w_gate)
    up = dot(x, w_up)
    sig = jax.nn.sigmoid(gate)
    active = gate * sig
    slope = up * sig * (1.0 + gate * (1.0 - sig))
    return active, slope, (active * up).astype(BF)


def act_kernel(x, home_gu, spare_gu, routes, acts, hidden, place_out):
    for p, place in enumerate(places_of(slots(), routes)):
        place_out[128 * p : 128 * p + 128, :] = place.astype(BF)
    for j, w in enumerate((home_gu, spare_gu)):
        active, slope, h = act(x[128 * j : 128 * j + 128, :], w[0], w[1])
        acts[128 * j : 128 * j + 128, :] = active
        acts[256 + 128 * j : 256 + 128 * j + 128, :] = slope
        hidden[128 * j : 128 * j + 128, :] = h


def pack_kernel(home_d, spare_d, home_gu, spare_gu, packed_out, packed, sems):
    there = 1024 * (1 - lax.axis_index("dp") % 2)
    rows = pl.ds(pl.multiple_of(there, 1024), 1024)
    copies = []
    for j, (w_d, w_gu) in enumerate(((home_d, home_gu), (spare_d, spare_gu))):
        for i in range(2):
            copies.append((w_gu.at[i, rows], packed.at[pl.ds(3072 * j + 1024 * i, 1024)]))
        for b in range(8):
            cols = pl.ds(pl.multiple_of(there + 128 * b, 128), 128)
            to = packed.at[pl.ds(3072 * j + 2048 + 128 * b, 128)]
            copies.append((w_d.at[:, cols], to))
    copies = [pltpu.make_async_copy(c[0], c[1], sems.at[i]) for i, c in enumerate(copies)]
    for copy in copies:
        copy.start()
    for copy in copies:
        copy.wait()
    store = pltpu.make_async_copy(packed, packed_out, sems.at[20])
    store.start()
    store.wait()


def sorted_rows(table, got, g):
    rows = dot(table, got[192 * g : 192 * g + 192, :]).astype(BF)
    for j in range(3):
        parts = [rows[64 * j + 16 * f : 64 * j + 16 * f + 16, :] for f in range(4)]
        yield 128 * j + 16 * g, jnp.concatenate(parts, axis=1)


def hidden_kernel(
    own_in, home_d, spare_d, packed, part_out, block_out, got, w_d, w_there, part, block, sems, outs
):
    here = half_at(lax.axis_index("dp") % 2)
    pairs = [(own_in, got)]
    for j, w in enumerate((home_d, spare_d)):
        pairs.append((w.at[:, here], w_d.at[j]))
        pairs.append((packed.at[pl.ds(3072 * j + 2048, 1024)], w_there.at[j]))
    loads = [pltpu.make_async_copy(a, b, sems.at[i]) for i, (a, b) in enumerate(pairs)]
    for load in loads:
        load.start()
    table = by_source(3)
    loads[0].wait()
    for g in range(GROUPS):
        for at, rows in sorted_rows(table, got, g):
            block[at : at + 16, :] = rows
    store = pltpu.make_async_copy(block, block_out, outs.at[0])
    store.start()
    for load in loads[1:]:
        load.wait()
    for j in range(2):
        mine = slice(128 * j, 128 * j + 128)
        there = [w_there[j, 128 * b : 128 * b + 128, :] for b in range(8)]
        weights = jnp.concatenate([w_d[j], jnp.concatenate(there, axis=1)])
        part[mine, :] = dot(block[mine, :], weights, NT)
    last = pltpu.make_async_copy(part, part_out, outs.at[1])
    last.start()
    last.wait()
    store.wait()


def rows_kernel(
    part_in,
    part_got,
    acts_in,
    acts_got,
    home_gu,
    spare_gu,
    packed,
    outgoing_out,
    grads_out,
    part,
    acts,
    w_gu,
    grads,
    rows,
    outgoing,
    sems,
    outs,
):
    here = half_at(lax.axis_index("dp") % 2)
    pairs = [
        (part_in, part.at[0]),
        (part_got, part.at[1]),
        (acts_in, acts.at[0]),
        (acts_got, acts.at[1]),
    ]
    for j, w in enumerate((home_gu, spare_gu)):
        for i in range(2):
            pairs.append((w.at[i, here], w_gu.at[j, i]))
            pairs.append((packed.at[pl.ds(3072 * j + 1024 * i, 1024)], w_gu.at[j, 2 + i]))
    loads = [pltpu.make_async_copy(a, b, sems.at[i]) for i, (a, b) in enumerate(pairs)]
    for load in loads:
        load.start()
    for load in loads[:4]:
        load.wait()
    for j in range(2):
        mine = pl.ds(128 * j, 128)
        slopes = pl.ds(256 + 128 * j, 128)
        both = []
        for k in range(2):
            hidden_grad = (
                part[0, mine, 128 * k : 128 * k + 128]
                + part[1, mine, 128 - 128 * k : 256 - 128 * k]
            )
            both.append((hidden_grad * acts[k, slopes, :]).astype(BF))
            both.append((hidden_grad * acts[k, mine, :]).astype(BF))
        grads[mine, :] = jnp.concatenate(both[:2], axis=1)
        for load in loads[4 + 4 * j : 8 + 4 * j]:
            load.wait()
        weights = jnp.concatenate([w_gu[j, i] for i in (0, 1, 2, 3)], axis=1)
        rows[mine, :] = dot(jnp.concatenate(both, axis=1), weights, NT).astype(BF)
    stores = [pltpu.make_async_copy(grads, grads_out, outs.at[0])]
    stores[0].start()
    table = by_source(2)
    for g in range(GROUPS):
        parts = []
        for j in range(2):
            at = slice(128 * j + 16 * g, 128 * j + 16 * g + 16)
            parts += [rows[at, 256 * f : 256 * f + 256] for f in range(4)]
        outgoing[128 * g : 128 * g + 128, :] = dot(table, jnp.concatenate(parts), TN).astype(BF)
        if g % 4 == 3:
            done = pl.ds(128 * (g - 3), 512)
            store = pltpu.make_async_copy(
                outgoing.at[done], outgoing_out.at[done], outs.at[1 + g // 4]
            )
            store.start()
            stores.append(store)
    for store in stores:
        store.wait()


def combine_kernel(returned, place, mine, low, rows):
    table = by_slot()
    for g in range(GROUPS):
        back = dot(table, returned[128 * g : 128 * g + 128, :], TN).astype(BF)
        for p in range(2):
            rows[128 * p + 16 * g : 128 * p + 16 * g + 16, :] = jnp.concatenate(
                [back[16 * (4 * p + f) : 16 * (4 * p + f) + 16, :] for f in range(4)], axis=1
            )
    total = dot(place[...], rows[...], TN)
    mine[...] = total
    low[...] = total.astype(BF)


def weights_kernel(
    experts,
    x,
    x_own,
    x_other,
    block_own,
    other,
    grads,
    hidden,
    home_gu,
    home_d,
    grad_gu,
    grad_d,
    x_prior,
    block,
):
    core = lax.axis_index("dp") % 2
    block[:, half_at(core)] = block_own[...]
    table = by_source(3)
    for g in range(GROUPS):
        for at, rows in sorted_rows(table, other, g):
            block[at : at + 16, half_at(1 - core)] = rows
    x_prior[pl.ds(pl.multiple_of(64 * core, 64), 64), :] = x_own[...]
    x_prior[pl.ds(pl.multiple_of(64 - 64 * core, 64), 64), :] = x_other[...]
    column = lax.axis_index("ep")
    keeps_own = experts[column] == column
    takes_prior = (column > 0) & (experts[jnp.maximum(column - 1, 0)] == column)
    active, slope, hidden_prior = act(x_prior[...], home_gu[0], home_gu[1])
    hidden_grad = dot(block[256:384, :], home_d[...], NT)
    grads_prior = jnp.concatenate(
        [(hidden_grad * slope).astype(BF), (hidden_grad * active).astype(BF)], axis=1
    )

    def only(keep, array):
        return jnp.where(keep, array, jnp.zeros_like(array))

    grads_spare = only(keeps_own, grads[128:256, :])
    grads_prior = only(takes_prior, grads_prior)
    hidden_spare = only(keeps_own, hidden[128:256, :])
    hidden_prior = only(takes_prior, hidden_prior)
    all_grads = jnp.concatenate([grads[0:128, :], grads_spare, grads_prior])
    all_hidden = jnp.concatenate([hidden[0:128, :], hidden_spare, hidden_prior])
    for i in range(8):
        at = slice(256 * i, 256 * i + 256)
        rows = jnp.concatenate([x[:, at], x_prior[:, at]])
        total = dot(rows, all_grads, TN).astype(BF)
        grad_gu[0, at, :] = total[:, :128]
        grad_gu[1, at, :] = total[:, 128:]
        grad_d[:, at] = dot(all_hidden, block[:, at], TN).astype(BF)


def finish_kernel(own, other, result):
    core = lax.axis_index("dp") % 2
    result[:, half_at(core)] = own[...]
    result[:, half_at(1 - core)] = other[...]


def shape(dims, kind=BF):
    return jax.ShapeDtypeStruct(dims, kind)


def call(kernel, outs, flops, nbytes, specs, scratch=(), into=None, vmem=60):
    return pl.pallas_call(
        kernel,
        out_shape=outs,
        in_specs=specs,
        out_specs=jax.tree.map(lambda _: VMEM, outs) if into is None else into,
        scratch_shapes=scratch,
        cost_estimate=pl.CostEstimate(flops=flops, bytes_accessed=nbytes, transcendentals=0),
        compiler_params=pltpu.CompilerParams(vmem_limit_bytes=vmem << 20),
    )


def on_device(
    out_grad,
    route_probs,
    routes,
    replica_expert,
    saved_inputs,
    home_gate_up,
    home_down,
    replica_gate_up,
    replica_down,
):
    home_gu, home_d = home_gate_up[0], home_down[0]
    spare_gu, spare_d = replica_gate_up[0], replica_down[0]

    core = lax.axis_index("dp") % 2
    x_part = lax.dynamic_slice_in_dim(saved_inputs[0, 1], core * 32, 32, 0)
    x_part, routes, route_probs = lax.optimization_barrier((x_part, routes, route_probs))
    x_part = to_next(x_part)

    outgoing = call(
        prep_kernel,
        shape((1536, 256)),
        10**6,
        10**6,
        [VMEM] * 3,
        [pltpu.VMEM((1536, 256), BF), pltpu.SemaphoreType.DMA((4,))],
        ANY,
    )(routes.T, route_probs.T, out_grad)
    incoming = exchange(outgoing)

    saved, _ = lax.optimization_barrier((saved_inputs, outgoing))
    x = saved.reshape(256, 2048)
    acts, hidden, place = call(
        act_kernel,
        (shape((512, 128), F32), shape((256, 128)), shape((256, 16))),
        10**11,
        4 * 10**6,
        [VMEM] * 4,
    )(x, home_gu, spare_gu, routes.T)
    weights, _ = lax.optimization_barrier(((home_d, spare_d, home_gu, spare_gu), outgoing))
    packed = call(
        pack_kernel,
        shape((6144, 128)),
        10**6,
        10**6,
        [ANY] * 4,
        [pltpu.VMEM((6144, 128), BF), pltpu.SemaphoreType.DMA((21,))],
        ANY,
    )(*weights)
    packed = swap_cores(packed)
    acts_got = swap_cores(acts)
    incoming, acts, x_part, packed, acts_got = lax.optimization_barrier(
        (incoming, acts, x_part, packed, acts_got)
    )

    part, block_own = call(
        hidden_kernel,
        (shape((256, 256), F32), shape((384, 1024))),
        10**9,
        4 * 10**6,
        [ANY] * 4,
        [
            pltpu.VMEM((1536, 256), BF),
            pltpu.VMEM((2, 128, 1024), BF),
            pltpu.VMEM((2, 1024, 128), BF),
            pltpu.VMEM((256, 256), F32),
            pltpu.VMEM((384, 1024), BF),
            pltpu.SemaphoreType.DMA((5,)),
            pltpu.SemaphoreType.DMA((2,)),
        ],
        (ANY, ANY),
    )(incoming, home_d, spare_d, packed)
    pair, grads = call(
        rows_kernel,
        (shape((1024, 256)), shape((256, 256))),
        10**9,
        4 * 10**6,
        [ANY] * 7,
        [
            pltpu.VMEM((2, 256, 256), F32),
            pltpu.VMEM((2, 512, 128), F32),
            pltpu.VMEM((2, 4, 1024, 128), BF),
            pltpu.VMEM((256, 256), BF),
            pltpu.VMEM((256, 1024), BF),
            pltpu.VMEM((1024, 256), BF),
            pltpu.SemaphoreType.DMA((12,)),
            pltpu.SemaphoreType.DMA((3,)),
        ],
        (ANY, ANY),
    )(part, swap_cores(part), acts, acts_got, home_gu, spare_gu, packed)
    returned = exchange(pair)

    x_part, incoming, _ = lax.optimization_barrier((x_part, incoming, pair))
    grad_gu, grad_d = call(
        weights_kernel,
        (shape((2, 2048, 128)), shape((128, 2048))),
        10**8,
        10**6,
        [SMEM] + [VMEM] * 9,
        [pltpu.VMEM((128, 2048), BF), pltpu.VMEM((384, 2048), BF)],
    )(
        replica_expert,
        x,
        x_part.reshape(64, 2048),
        swap_cores(x_part).reshape(64, 2048),
        block_own,
        swap_cores(incoming),
        grads,
        hidden,
        home_gu,
        home_d,
    )
    returned, grad_gu = lax.optimization_barrier((returned, grad_gu))

    mine, low = call(
        combine_kernel,
        (shape((16, 1024), F32), shape((16, 1024))),
        10**8,
        10**6,
        [VMEM] * 2,
        [pltpu.VMEM((256, 1024), BF)],
        vmem=28,
    )(returned, place)
    one = along_dp(low, lambda z: (z // 3 * 3 + (z + 1) % 3, 0))
    two = along_dp(low, lambda z: (z // 3 * 3 + (z + 2) % 3, 0))
    total = mine + one.astype(F32) + two.astype(F32)
    total = (total + along_dp(total.astype(BF), lambda z: ((z + 3) % 6, 0)).astype(F32)).astype(BF)
    input_grad = call(finish_kernel, shape((16, 2048)), 10**3, 10**5, [VMEM] * 2, vmem=28)(
        total, swap_cores(total)
    )
    return (input_grad, grad_gu[None], grad_d[None])


def solution(mesh):
    placed = (
        P("ep", None),
        P("ep", None),
        P("ep", None),
        P(),
        P("ep", None, None, None, None),
        P("ep", None, None, "dp"),
        P("ep", "dp", None),
        P("ep", None, None, "dp"),
        P("ep", "dp", None),
    )
    return jax.shard_map(
        on_device,
        mesh=mesh,
        in_specs=placed,
        out_specs=(P("ep", None), P("ep", None, None, "dp"), P("ep", "dp", None)),
        check_vma=False,
    )
```

```python
import jax
import jax.numpy as jnp
from jax import lax
from jax.experimental import pallas as pl
from jax.experimental.pallas import tpu as pltpu
from jax.sharding import PartitionSpec as P

BF = jnp.bfloat16
F32 = jnp.float32
NT = (((1,), (1,)), ((), ()))
TN = (((0,), (0,)), ((), ()))
GROUPS = 8
VMEM = pl.BlockSpec(memory_space=pltpu.VMEM)
ANY = pl.BlockSpec(memory_space=pl.ANY)
HBM = pl.BlockSpec(memory_space=pltpu.HBM)
SMEM = pl.BlockSpec(memory_space=pltpu.SMEM)


def along_dp(array, to):
    pairs = [(2 * z + c, 2 * to(z)[0] + (c ^ to(z)[1])) for z in range(6) for c in range(2)]
    return lax.ppermute(array, "dp", pairs)


def swap_cores(array):
    return along_dp(array, lambda z: (z, 1))


def mirrored(e, dp):
    return 12 * e + (dp if e % 2 == 0 else 10 - dp + 2 * (dp % 2))


def to_next(array):
    length = lax.axis_size("ep")
    pairs = [
        (mirrored(e, dp), mirrored(e + 1, dp)) for e in range(length - 1) for dp in range(12)
    ]
    return lax.ppermute(array, ("ep", "dp"), pairs)


def exchange(array):
    length = lax.axis_size("ep")
    groups = [[mirrored(e, dp) for e in range(length)] for dp in range(12)]
    array = array.reshape(length, -1, 256)
    array = lax.all_to_all(
        array, ("ep", "dp"), split_axis=0, concat_axis=0, axis_index_groups=groups, tiled=True
    )
    return array.reshape(-1, 256)


def dot(a, b, dims=(((1,), (0,)), ((), ()))):
    return lax.dot_general(a, b, dims, preferred_element_type=F32)


def half_at(core):
    return pl.ds(pl.multiple_of(core * 1024, 1024), 1024)


def by_slot():
    row = lax.broadcasted_iota(jnp.int32, (128, 128), 0)
    col = lax.broadcasted_iota(jnp.int32, (128, 128), 1)
    return (col == 16 * (row % 8) + 2 * (row // 16) + row // 8 % 2).astype(F32).astype(BF)


def by_source(kinds):
    row = lax.broadcasted_iota(jnp.int32, (64 * kinds, 64 * kinds), 0)
    col = lax.broadcasted_iota(jnp.int32, (64 * kinds, 64 * kinds), 1)
    want = 8 * kinds * (row // 2 % 8) + 8 * (row // 64) + 4 * (row % 2) + row // 16 % 4
    return (col == want).astype(F32).astype(BF)


def by_prior():
    row = lax.broadcasted_iota(jnp.int32, (128, 128), 0)
    col = lax.broadcasted_iota(jnp.int32, (128, 128), 1)
    return (col == 16 * (row % 8) + row // 8).astype(F32).astype(BF)


def slots():
    return lax.broadcasted_iota(jnp.int32, (128, 16), 0)


def places_of(slot, routes):
    named = jnp.zeros(slot.shape, F32)
    for k in range(8):
        named = named + jnp.where(slot == routes[k : k + 1, :], 1.0, 0.0)
    before = lax.broadcasted_iota(jnp.int32, (16, 16), 0) < lax.broadcasted_iota(
        jnp.int32, (16, 16), 1
    )
    earlier = dot(named.astype(BF), before.astype(F32).astype(BF))
    return [jnp.where(earlier == p, named, 0.0) for p in range(2)]


def routed(slot, routes, probs, half):
    prob = jnp.zeros(slot.shape, F32)
    for k in range(8):
        prob = prob + jnp.where(slot == routes[k : k + 1, :], probs[k : k + 1, :], 0.0)
    places = places_of(slot, routes)
    rows = []
    for place in places:
        row_prob = jnp.sum(place * prob, axis=1, keepdims=True)
        rows.append((dot(place.astype(BF), half) * row_prob).astype(BF))
    return places, rows


def blocks_of(rows, g):
    parts = [
        rows[p][16 * g : 16 * g + 16, 256 * f : 256 * f + 256] for p in range(2) for f in range(4)
    ]
    return jnp.concatenate(parts)


def part_kernel(saved, part, sem):
    first = 32 * (lax.axis_index("dp") % 2)
    copy = pltpu.make_async_copy(saved.at[0, 1, pl.ds(first, 32)], part, sem)
    copy.start()
    copy.wait()


def prep_kernel(routes, probs, out_grad, outgoing_out, outgoing, sems):
    stores = []
    half = out_grad[:, half_at(lax.axis_index("dp") % 2)]
    table = by_slot()
    _, rows = routed(slots(), routes, probs, half)
    prior = 2 * lax.broadcasted_iota(jnp.int32, (64, 16), 0) - 1
    _, prior_rows = routed(prior, routes, probs, half)
    prior_table = by_prior()
    for g in range(4):
        held = [dot(table, blocks_of(rows, 2 * g + h)).astype(BF) for h in range(2)]
        extra = dot(prior_table, blocks_of(prior_rows, g)).astype(BF)
        for h in range(2):
            for c in range(8):
                at = 24 * (16 * g + 8 * h + c)
                outgoing[at : at + 16, :] = held[h][16 * c : 16 * c + 16, :]
                outgoing[at + 16 : at + 24, :] = extra[64 * h + 8 * c : 64 * h + 8 * c + 8, :]
        done = pl.ds(384 * g, 384)
        stores.append(
            pltpu.make_async_copy(outgoing.at[done], outgoing_out.at[done], sems.at[g])
        )
        stores[g].start()
    for store in stores:
        store.wait()


def act(x, w_gate, w_up):
    gate = dot(x, w_gate)
    up = dot(x, w_up)
    sig = jax.nn.sigmoid(gate)
    active = gate * sig
    slope = up * sig * (1.0 + gate * (1.0 - sig))
    return active, slope, (active * up).astype(BF)


def act_kernel(x, home_gu, spare_gu, routes, acts, hidden, place_out):
    for p, place in enumerate(places_of(slots(), routes)):
        place_out[128 * p : 128 * p + 128, :] = place.astype(BF)
    for j, w in enumerate((home_gu, spare_gu)):
        active, slope, h = act(x[128 * j : 128 * j + 128, :], w[0], w[1])
        acts[128 * j : 128 * j + 128, :] = active
        acts[256 + 128 * j : 256 + 128 * j + 128, :] = slope
        hidden[128 * j : 128 * j + 128, :] = h


def pack_kernel(home_d, spare_d, home_gu, spare_gu, packed_out, packed, sems):
    there = 1024 * (1 - lax.axis_index("dp") % 2)
    rows = pl.ds(pl.multiple_of(there, 1024), 1024)
    copies = []
    for j, (w_d, w_gu) in enumerate(((home_d, home_gu), (spare_d, spare_gu))):
        for i in range(2):
            copies.append((w_gu.at[i, rows], packed.at[pl.ds(3072 * j + 1024 * i, 1024)]))
        for b in range(8):
            cols = pl.ds(pl.multiple_of(there + 128 * b, 128), 128)
            to = packed.at[pl.ds(3072 * j + 2048 + 128 * b, 128)]
            copies.append((w_d.at[:, cols], to))
    copies = [pltpu.make_async_copy(c[0], c[1], sems.at[i]) for i, c in enumerate(copies)]
    for copy in copies:
        copy.start()
    for copy in copies:
        copy.wait()
    store = pltpu.make_async_copy(packed, packed_out, sems.at[20])
    store.start()
    store.wait()


def sorted_rows(table, got, g):
    rows = dot(table, got[192 * g : 192 * g + 192, :]).astype(BF)
    for j in range(3):
        parts = [rows[64 * j + 16 * f : 64 * j + 16 * f + 16, :] for f in range(4)]
        yield 128 * j + 16 * g, jnp.concatenate(parts, axis=1)


def hidden_kernel(
    own_in, home_d, spare_d, packed, part_out, block_out, got, w_d, w_there, part, block, sems, outs
):
    here = half_at(lax.axis_index("dp") % 2)
    pairs = [(own_in, got)]
    for j, w in enumerate((home_d, spare_d)):
        pairs.append((w.at[:, here], w_d.at[j]))
        pairs.append((packed.at[pl.ds(3072 * j + 2048, 1024)], w_there.at[j]))
    loads = [pltpu.make_async_copy(a, b, sems.at[i]) for i, (a, b) in enumerate(pairs)]
    for load in loads:
        load.start()
    table = by_source(3)
    loads[0].wait()
    for g in range(GROUPS):
        for at, rows in sorted_rows(table, got, g):
            block[at : at + 16, :] = rows
    store = pltpu.make_async_copy(block, block_out, outs.at[0])
    store.start()
    for load in loads[1:]:
        load.wait()
    for j in range(2):
        mine = slice(128 * j, 128 * j + 128)
        there = [w_there[j, 128 * b : 128 * b + 128, :] for b in range(8)]
        weights = jnp.concatenate([w_d[j], jnp.concatenate(there, axis=1)])
        part[mine, :] = dot(block[mine, :], weights, NT)
    last = pltpu.make_async_copy(part, part_out, outs.at[1])
    last.start()
    last.wait()
    store.wait()


def rows_kernel(
    part_in,
    part_got,
    acts_in,
    acts_got,
    home_gu,
    spare_gu,
    packed,
    outgoing_out,
    grads_out,
    part,
    acts,
    w_gu,
    grads,
    rows,
    outgoing,
    sems,
    outs,
):
    here = half_at(lax.axis_index("dp") % 2)
    pairs = [
        (part_in, part.at[0]),
        (part_got, part.at[1]),
        (acts_in, acts.at[0]),
        (acts_got, acts.at[1]),
    ]
    for j, w in enumerate((home_gu, spare_gu)):
        for i in range(2):
            pairs.append((w.at[i, here], w_gu.at[j, i]))
            pairs.append((packed.at[pl.ds(3072 * j + 1024 * i, 1024)], w_gu.at[j, 2 + i]))
    loads = [pltpu.make_async_copy(a, b, sems.at[i]) for i, (a, b) in enumerate(pairs)]
    for load in loads:
        load.start()
    for load in loads[:4]:
        load.wait()
    for j in range(2):
        mine = pl.ds(128 * j, 128)
        slopes = pl.ds(256 + 128 * j, 128)
        both = []
        for k in range(2):
            hidden_grad = (
                part[0, mine, 128 * k : 128 * k + 128]
                + part[1, mine, 128 - 128 * k : 256 - 128 * k]
            )
            both.append((hidden_grad * acts[k, slopes, :]).astype(BF))
            both.append((hidden_grad * acts[k, mine, :]).astype(BF))
        grads[mine, :] = jnp.concatenate(both[:2], axis=1)
        for load in loads[4 + 4 * j : 8 + 4 * j]:
            load.wait()
        weights = jnp.concatenate([w_gu[j, i] for i in (0, 1, 2, 3)], axis=1)
        rows[mine, :] = dot(jnp.concatenate(both, axis=1), weights, NT).astype(BF)
    stores = [pltpu.make_async_copy(grads, grads_out, outs.at[0])]
    stores[0].start()
    table = by_source(2)
    for g in range(GROUPS):
        parts = []
        for j in range(2):
            at = slice(128 * j + 16 * g, 128 * j + 16 * g + 16)
            parts += [rows[at, 256 * f : 256 * f + 256] for f in range(4)]
        outgoing[128 * g : 128 * g + 128, :] = dot(table, jnp.concatenate(parts), TN).astype(BF)
        if g % 4 == 3:
            done = pl.ds(128 * (g - 3), 512)
            store = pltpu.make_async_copy(
                outgoing.at[done], outgoing_out.at[done], outs.at[1 + g // 4]
            )
            store.start()
            stores.append(store)
    for store in stores:
        store.wait()


def combine_kernel(returned, place, mine, low, rows):
    table = by_slot()
    for g in range(GROUPS):
        back = dot(table, returned[128 * g : 128 * g + 128, :], TN).astype(BF)
        for p in range(2):
            rows[128 * p + 16 * g : 128 * p + 16 * g + 16, :] = jnp.concatenate(
                [back[16 * (4 * p + f) : 16 * (4 * p + f) + 16, :] for f in range(4)], axis=1
            )
    total = dot(place[...], rows[...], TN)
    mine[...] = total
    low[...] = total.astype(BF)


def weights_kernel(
    experts,
    x,
    x_own,
    x_other,
    block_own,
    other,
    grads,
    hidden,
    home_gu,
    home_d,
    grad_gu,
    grad_d,
    x_prior,
    block,
):
    core = lax.axis_index("dp") % 2
    block[:, half_at(core)] = block_own[...]
    table = by_source(3)
    for g in range(GROUPS):
        for at, rows in sorted_rows(table, other, g):
            block[at : at + 16, half_at(1 - core)] = rows
    x_prior[pl.ds(pl.multiple_of(64 * core, 64), 64), :] = x_own[...]
    x_prior[pl.ds(pl.multiple_of(64 - 64 * core, 64), 64), :] = x_other[...]
    column = lax.axis_index("ep")
    keeps_own = experts[column] == column
    takes_prior = (column > 0) & (experts[jnp.maximum(column - 1, 0)] == column)
    active, slope, hidden_prior = act(x_prior[...], home_gu[0], home_gu[1])
    hidden_grad = dot(block[256:384, :], home_d[...], NT)
    grads_prior = jnp.concatenate(
        [(hidden_grad * slope).astype(BF), (hidden_grad * active).astype(BF)], axis=1
    )

    def only(keep, array):
        return jnp.where(keep, array, jnp.zeros_like(array))

    grads_spare = only(keeps_own, grads[128:256, :])
    grads_prior = only(takes_prior, grads_prior)
    hidden_spare = only(keeps_own, hidden[128:256, :])
    hidden_prior = only(takes_prior, hidden_prior)
    all_grads = jnp.concatenate([grads[0:128, :], grads_spare, grads_prior])
    all_hidden = jnp.concatenate([hidden[0:128, :], hidden_spare, hidden_prior])
    for i in range(8):
        at = slice(256 * i, 256 * i + 256)
        rows = jnp.concatenate([x[:, at], x_prior[:, at]])
        total = dot(rows, all_grads, TN).astype(BF)
        grad_gu[0, at, :] = total[:, :128]
        grad_gu[1, at, :] = total[:, 128:]
        grad_d[:, at] = dot(all_hidden, block[:, at], TN).astype(BF)


def finish_kernel(own, other, result):
    core = lax.axis_index("dp") % 2
    result[:, half_at(core)] = own[...]
    result[:, half_at(1 - core)] = other[...]


def shape(dims, kind=BF):
    return jax.ShapeDtypeStruct(dims, kind)


def call(kernel, outs, flops, nbytes, specs, scratch=(), into=None, vmem=60):
    return pl.pallas_call(
        kernel,
        out_shape=outs,
        in_specs=specs,
        out_specs=jax.tree.map(lambda _: VMEM, outs) if into is None else into,
        scratch_shapes=scratch,
        cost_estimate=pl.CostEstimate(flops=flops, bytes_accessed=nbytes, transcendentals=0),
        compiler_params=pltpu.CompilerParams(vmem_limit_bytes=vmem << 20),
    )


def on_device(
    out_grad,
    route_probs,
    routes,
    replica_expert,
    saved_inputs,
    home_gate_up,
    home_down,
    replica_gate_up,
    replica_down,
):
    home_gu, home_d = home_gate_up[0], home_down[0]
    spare_gu, spare_d = replica_gate_up[0], replica_down[0]

    x_part = call(
        part_kernel,
        shape((32, 2, 2048)),
        10**3,
        10**5,
        [ANY],
        [pltpu.SemaphoreType.DMA(())],
    )(saved_inputs)
    x_part, routes, route_probs = lax.optimization_barrier((x_part, routes, route_probs))
    x_part = to_next(x_part)

    outgoing = call(
        prep_kernel,
        shape((1536, 256)),
        10**6,
        10**6,
        [VMEM] * 3,
        [pltpu.VMEM((1536, 256), BF), pltpu.SemaphoreType.DMA((4,))],
        ANY,
    )(routes.T, route_probs.T, out_grad)
    incoming = exchange(outgoing)

    saved, _ = lax.optimization_barrier((saved_inputs, outgoing))
    x = saved.reshape(256, 2048)
    acts, hidden, place = call(
        act_kernel,
        (shape((512, 128), F32), shape((256, 128)), shape((256, 16))),
        10**11,
        4 * 10**6,
        [VMEM] * 4,
    )(x, home_gu, spare_gu, routes.T)
    weights, _ = lax.optimization_barrier(((home_d, spare_d, home_gu, spare_gu), outgoing))
    packed = call(
        pack_kernel,
        shape((6144, 128)),
        10**6,
        10**6,
        [ANY] * 4,
        [pltpu.VMEM((6144, 128), BF), pltpu.SemaphoreType.DMA((21,))],
        ANY,
    )(*weights)
    packed = swap_cores(packed)
    acts_got = swap_cores(acts)
    incoming, acts, x_part, packed, acts_got = lax.optimization_barrier(
        (incoming, acts, x_part, packed, acts_got)
    )

    part, block_own = call(
        hidden_kernel,
        (shape((256, 256), F32), shape((384, 1024))),
        10**9,
        4 * 10**6,
        [ANY] * 4,
        [
            pltpu.VMEM((1536, 256), BF),
            pltpu.VMEM((2, 128, 1024), BF),
            pltpu.VMEM((2, 1024, 128), BF),
            pltpu.VMEM((256, 256), F32),
            pltpu.VMEM((384, 1024), BF),
            pltpu.SemaphoreType.DMA((5,)),
            pltpu.SemaphoreType.DMA((2,)),
        ],
        (ANY, ANY),
        vmem=50,
    )(incoming, home_d, spare_d, packed)
    pair, grads = call(
        rows_kernel,
        (pltpu.HBM((1024, 256), BF), pltpu.HBM((256, 256), BF)),
        10**9,
        4 * 10**6,
        [ANY] * 7,
        [
            pltpu.VMEM((2, 256, 256), F32),
            pltpu.VMEM((2, 512, 128), F32),
            pltpu.VMEM((2, 4, 1024, 128), BF),
            pltpu.VMEM((256, 256), BF),
            pltpu.VMEM((256, 1024), BF),
            pltpu.VMEM((1024, 256), BF),
            pltpu.SemaphoreType.DMA((12,)),
            pltpu.SemaphoreType.DMA((3,)),
        ],
        (HBM, HBM),
        vmem=50,
    )(part, swap_cores(part), acts, acts_got, home_gu, spare_gu, packed)
    returned = exchange(pair)

    x_part, incoming, _ = lax.optimization_barrier((x_part, incoming, pair))
    grad_gu, grad_d = call(
        weights_kernel,
        (shape((2, 2048, 128)), shape((128, 2048))),
        10**8,
        10**6,
        [SMEM] + [VMEM] * 9,
        [pltpu.VMEM((128, 2048), BF), pltpu.VMEM((384, 2048), BF)],
    )(
        replica_expert,
        x,
        x_part.reshape(64, 2048),
        swap_cores(x_part).reshape(64, 2048),
        block_own,
        swap_cores(incoming),
        grads,
        hidden,
        home_gu,
        home_d,
    )
    returned, grad_gu = lax.optimization_barrier((returned, grad_gu))

    mine, low = call(
        combine_kernel,
        (shape((16, 1024), F32), shape((16, 1024))),
        10**8,
        10**6,
        [VMEM] * 2,
        [pltpu.VMEM((256, 1024), BF)],
        vmem=28,
    )(returned, place)
    one = along_dp(low, lambda z: (z // 3 * 3 + (z + 1) % 3, 0))
    two = along_dp(low, lambda z: (z // 3 * 3 + (z + 2) % 3, 0))
    total = mine + one.astype(F32) + two.astype(F32)
    total = (total + along_dp(total.astype(BF), lambda z: ((z + 3) % 6, 0)).astype(F32)).astype(BF)
    input_grad = call(finish_kernel, shape((16, 2048)), 10**3, 10**5, [VMEM] * 2, vmem=28)(
        total, swap_cores(total)
    )
    return (input_grad, grad_gu[None], grad_d[None])


def solution(mesh):
    placed = (
        P("ep", None),
        P("ep", None),
        P("ep", None),
        P(),
        P("ep", None, None, None, None),
        P("ep", None, None, "dp"),
        P("ep", "dp", None),
        P("ep", None, None, "dp"),
        P("ep", "dp", None),
    )
    return jax.shard_map(
        on_device,
        mesh=mesh,
        in_specs=placed,
        out_specs=(P("ep", None), P("ep", None, None, "dp"), P("ep", "dp", None)),
        check_vma=False,
    )
```

```python
import jax
import jax.numpy as jnp
from jax import lax
from jax.experimental import pallas as pl
from jax.experimental.pallas import tpu as pltpu
from jax.sharding import PartitionSpec as P

BF = jnp.bfloat16
F32 = jnp.float32
NT = (((1,), (1,)), ((), ()))
TN = (((0,), (0,)), ((), ()))
GROUPS = 8
VMEM = pl.BlockSpec(memory_space=pltpu.VMEM)
ANY = pl.BlockSpec(memory_space=pl.ANY)
HBM = pl.BlockSpec(memory_space=pltpu.HBM)
SMEM = pl.BlockSpec(memory_space=pltpu.SMEM)


def along_dp(array, to):
    pairs = [(2 * z + c, 2 * to(z)[0] + (c ^ to(z)[1])) for z in range(6) for c in range(2)]
    return lax.ppermute(array, "dp", pairs)


def swap_cores(array):
    return along_dp(array, lambda z: (z, 1))


def mirrored(e, dp):
    return 12 * e + (dp if e % 2 == 0 else 10 - dp + 2 * (dp % 2))


def to_next(array):
    length = lax.axis_size("ep")
    pairs = [
        (mirrored(e, dp), mirrored(e + 1, dp)) for e in range(length - 1) for dp in range(12)
    ]
    return lax.ppermute(array, ("ep", "dp"), pairs)


def exchange(array):
    length = lax.axis_size("ep")
    groups = [[mirrored(e, dp) for e in range(length)] for dp in range(12)]
    array = array.reshape(length, -1, 256)
    array = lax.all_to_all(
        array, ("ep", "dp"), split_axis=0, concat_axis=0, axis_index_groups=groups, tiled=True
    )
    return array.reshape(-1, 256)


def dot(a, b, dims=(((1,), (0,)), ((), ()))):
    return lax.dot_general(a, b, dims, preferred_element_type=F32)


def half_at(core):
    return pl.ds(pl.multiple_of(core * 1024, 1024), 1024)


def by_slot():
    row = lax.broadcasted_iota(jnp.int32, (128, 128), 0)
    col = lax.broadcasted_iota(jnp.int32, (128, 128), 1)
    return (col == 16 * (row % 8) + 2 * (row // 16) + row // 8 % 2).astype(F32).astype(BF)


def by_source(kinds):
    row = lax.broadcasted_iota(jnp.int32, (64 * kinds, 64 * kinds), 0)
    col = lax.broadcasted_iota(jnp.int32, (64 * kinds, 64 * kinds), 1)
    want = 8 * kinds * (row // 2 % 8) + 8 * (row // 64) + 4 * (row % 2) + row // 16 % 4
    return (col == want).astype(F32).astype(BF)


def by_prior():
    row = lax.broadcasted_iota(jnp.int32, (128, 128), 0)
    col = lax.broadcasted_iota(jnp.int32, (128, 128), 1)
    return (col == 16 * (row % 8) + row // 8).astype(F32).astype(BF)


def slots():
    return lax.broadcasted_iota(jnp.int32, (128, 16), 0)


def places_of(slot, routes):
    named = jnp.zeros(slot.shape, F32)
    for k in range(8):
        named = named + jnp.where(slot == routes[k : k + 1, :], 1.0, 0.0)
    before = lax.broadcasted_iota(jnp.int32, (16, 16), 0) < lax.broadcasted_iota(
        jnp.int32, (16, 16), 1
    )
    earlier = dot(named.astype(BF), before.astype(F32).astype(BF))
    return [jnp.where(earlier == p, named, 0.0) for p in range(2)]


def routed(slot, routes, probs, half):
    prob = jnp.zeros(slot.shape, F32)
    for k in range(8):
        prob = prob + jnp.where(slot == routes[k : k + 1, :], probs[k : k + 1, :], 0.0)
    places = places_of(slot, routes)
    rows = []
    for place in places:
        row_prob = jnp.sum(place * prob, axis=1, keepdims=True)
        rows.append((dot(place.astype(BF), half) * row_prob).astype(BF))
    return places, rows


def blocks_of(rows, g):
    parts = [
        rows[p][16 * g : 16 * g + 16, 256 * f : 256 * f + 256] for p in range(2) for f in range(4)
    ]
    return jnp.concatenate(parts)


def part_kernel(saved, part, sem):
    first = 32 * (lax.axis_index("dp") % 2)
    copy = pltpu.make_async_copy(saved.at[0, 1, pl.ds(first, 32)], part, sem)
    copy.start()
    copy.wait()


def prep_kernel(routes, probs, out_grad, outgoing_out, outgoing, sems):
    stores = []
    half = out_grad[:, half_at(lax.axis_index("dp") % 2)]
    table = by_slot()
    _, rows = routed(slots(), routes, probs, half)
    prior = 2 * lax.broadcasted_iota(jnp.int32, (64, 16), 0) - 1
    _, prior_rows = routed(prior, routes, probs, half)
    prior_table = by_prior()
    for g in range(4):
        held = [dot(table, blocks_of(rows, 2 * g + h)).astype(BF) for h in range(2)]
        extra = dot(prior_table, blocks_of(prior_rows, g)).astype(BF)
        for h in range(2):
            for c in range(8):
                at = 24 * (16 * g + 8 * h + c)
                outgoing[at : at + 16, :] = held[h][16 * c : 16 * c + 16, :]
                outgoing[at + 16 : at + 24, :] = extra[64 * h + 8 * c : 64 * h + 8 * c + 8, :]
        done = pl.ds(384 * g, 384)
        stores.append(
            pltpu.make_async_copy(outgoing.at[done], outgoing_out.at[done], sems.at[g])
        )
        stores[g].start()
    for store in stores:
        store.wait()


def act(x, w_gate, w_up):
    gate = dot(x, w_gate)
    up = dot(x, w_up)
    sig = jax.nn.sigmoid(gate)
    active = gate * sig
    slope = up * sig * (1.0 + gate * (1.0 - sig))
    return active, slope, (active * up).astype(BF)


def act_kernel(x, home_gu, spare_gu, routes, acts, hidden, place_out):
    for p, place in enumerate(places_of(slots(), routes)):
        place_out[128 * p : 128 * p + 128, :] = place.astype(BF)
    for j, w in enumerate((home_gu, spare_gu)):
        active, slope, h = act(x[128 * j : 128 * j + 128, :], w[0], w[1])
        acts[128 * j : 128 * j + 128, :] = active
        acts[256 + 128 * j : 256 + 128 * j + 128, :] = slope
        hidden[128 * j : 128 * j + 128, :] = h


def pack_kernel(home_d, spare_d, home_gu, spare_gu, packed_out, packed, sems):
    there = 1024 * (1 - lax.axis_index("dp") % 2)
    rows = pl.ds(pl.multiple_of(there, 1024), 1024)
    copies = []
    for j, (w_d, w_gu) in enumerate(((home_d, home_gu), (spare_d, spare_gu))):
        for i in range(2):
            copies.append((w_gu.at[i, rows], packed.at[pl.ds(3072 * j + 1024 * i, 1024)]))
        for b in range(8):
            cols = pl.ds(pl.multiple_of(there + 128 * b, 128), 128)
            to = packed.at[pl.ds(3072 * j + 2048 + 128 * b, 128)]
            copies.append((w_d.at[:, cols], to))
    copies = [pltpu.make_async_copy(c[0], c[1], sems.at[i]) for i, c in enumerate(copies)]
    for copy in copies:
        copy.start()
    for copy in copies:
        copy.wait()
    store = pltpu.make_async_copy(packed, packed_out, sems.at[20])
    store.start()
    store.wait()


def sorted_rows(table, got, g):
    rows = dot(table, got[192 * g : 192 * g + 192, :]).astype(BF)
    for j in range(3):
        parts = [rows[64 * j + 16 * f : 64 * j + 16 * f + 16, :] for f in range(4)]
        yield 128 * j + 16 * g, jnp.concatenate(parts, axis=1)


def hidden_kernel(
    own_in, home_d, spare_d, packed, part_out, block_out, got, w_d, w_there, part, block, sems, outs
):
    here = half_at(lax.axis_index("dp") % 2)
    pairs = [(own_in, got)]
    for j, w in enumerate((home_d, spare_d)):
        pairs.append((w.at[:, here], w_d.at[j]))
        pairs.append((packed.at[pl.ds(3072 * j + 2048, 1024)], w_there.at[j]))
    loads = [pltpu.make_async_copy(a, b, sems.at[i]) for i, (a, b) in enumerate(pairs)]
    for load in loads:
        load.start()
    table = by_source(3)
    loads[0].wait()
    for g in range(GROUPS):
        for at, rows in sorted_rows(table, got, g):
            block[at : at + 16, :] = rows
    store = pltpu.make_async_copy(block, block_out, outs.at[0])
    store.start()
    for load in loads[1:]:
        load.wait()
    for j in range(2):
        mine = slice(128 * j, 128 * j + 128)
        there = [w_there[j, 128 * b : 128 * b + 128, :] for b in range(8)]
        weights = jnp.concatenate([w_d[j], jnp.concatenate(there, axis=1)])
        part[mine, :] = dot(block[mine, :], weights, NT)
    last = pltpu.make_async_copy(part, part_out, outs.at[1])
    last.start()
    last.wait()
    store.wait()


def rows_kernel(
    part_in,
    part_got,
    acts_in,
    acts_got,
    home_gu,
    spare_gu,
    packed,
    outgoing_out,
    grads_out,
    part,
    acts,
    w_gu,
    grads,
    rows,
    outgoing,
    sems,
    outs,
):
    here = half_at(lax.axis_index("dp") % 2)
    pairs = [
        (part_in, part.at[0]),
        (part_got, part.at[1]),
        (acts_in, acts.at[0]),
        (acts_got, acts.at[1]),
    ]
    for j, w in enumerate((home_gu, spare_gu)):
        for i in range(2):
            pairs.append((w.at[i, here], w_gu.at[j, i]))
            pairs.append((packed.at[pl.ds(3072 * j + 1024 * i, 1024)], w_gu.at[j, 2 + i]))
    loads = [pltpu.make_async_copy(a, b, sems.at[i]) for i, (a, b) in enumerate(pairs)]
    for load in loads:
        load.start()
    for load in loads[:4]:
        load.wait()
    for j in range(2):
        mine = pl.ds(128 * j, 128)
        slopes = pl.ds(256 + 128 * j, 128)
        both = []
        for k in range(2):
            hidden_grad = (
                part[0, mine, 128 * k : 128 * k + 128]
                + part[1, mine, 128 - 128 * k : 256 - 128 * k]
            )
            both.append((hidden_grad * acts[k, slopes, :]).astype(BF))
            both.append((hidden_grad * acts[k, mine, :]).astype(BF))
        grads[mine, :] = jnp.concatenate(both[:2], axis=1)
        for load in loads[4 + 4 * j : 8 + 4 * j]:
            load.wait()
        weights = jnp.concatenate([w_gu[j, i] for i in (0, 1, 2, 3)], axis=1)
        rows[mine, :] = dot(jnp.concatenate(both, axis=1), weights, NT).astype(BF)
    stores = [pltpu.make_async_copy(grads, grads_out, outs.at[0])]
    stores[0].start()
    table = by_source(2)
    for g in range(GROUPS):
        parts = []
        for j in range(2):
            at = slice(128 * j + 16 * g, 128 * j + 16 * g + 16)
            parts += [rows[at, 256 * f : 256 * f + 256] for f in range(4)]
        outgoing[128 * g : 128 * g + 128, :] = dot(table, jnp.concatenate(parts), TN).astype(BF)
        if g % 4 == 3:
            done = pl.ds(128 * (g - 3), 512)
            store = pltpu.make_async_copy(
                outgoing.at[done], outgoing_out.at[done], outs.at[1 + g // 4]
            )
            store.start()
            stores.append(store)
    for store in stores:
        store.wait()


def combine_kernel(returned, place, mine, low, rows):
    table = by_slot()
    for g in range(GROUPS):
        back = dot(table, returned[128 * g : 128 * g + 128, :], TN).astype(BF)
        for p in range(2):
            rows[128 * p + 16 * g : 128 * p + 16 * g + 16, :] = jnp.concatenate(
                [back[16 * (4 * p + f) : 16 * (4 * p + f) + 16, :] for f in range(4)], axis=1
            )
    total = dot(place[...], rows[...], TN)
    mine[...] = total
    low[...] = total.astype(BF)


def weights_kernel(
    experts,
    x,
    x_own,
    x_other,
    block_own,
    other,
    grads,
    hidden,
    home_gu,
    home_d,
    grad_gu,
    grad_d,
    x_prior,
    block,
):
    core = lax.axis_index("dp") % 2
    block[:, half_at(core)] = block_own[...]
    table = by_source(3)
    for g in range(GROUPS):
        for at, rows in sorted_rows(table, other, g):
            block[at : at + 16, half_at(1 - core)] = rows
    x_prior[pl.ds(pl.multiple_of(64 * core, 64), 64), :] = x_own[...]
    x_prior[pl.ds(pl.multiple_of(64 - 64 * core, 64), 64), :] = x_other[...]
    column = lax.axis_index("ep")
    keeps_own = experts[column] == column
    takes_prior = (column > 0) & (experts[jnp.maximum(column - 1, 0)] == column)
    active, slope, hidden_prior = act(x_prior[...], home_gu[0], home_gu[1])
    hidden_grad = dot(block[256:384, :], home_d[...], NT)
    grads_prior = jnp.concatenate(
        [(hidden_grad * slope).astype(BF), (hidden_grad * active).astype(BF)], axis=1
    )

    def only(keep, array):
        return jnp.where(keep, array, jnp.zeros_like(array))

    grads_spare = only(keeps_own, grads[128:256, :])
    grads_prior = only(takes_prior, grads_prior)
    hidden_spare = only(keeps_own, hidden[128:256, :])
    hidden_prior = only(takes_prior, hidden_prior)
    all_grads = jnp.concatenate([grads[0:128, :], grads_spare, grads_prior])
    all_hidden = jnp.concatenate([hidden[0:128, :], hidden_spare, hidden_prior])
    for i in range(8):
        at = slice(256 * i, 256 * i + 256)
        rows = jnp.concatenate([x[:, at], x_prior[:, at]])
        total = dot(rows, all_grads, TN).astype(BF)
        grad_gu[0, at, :] = total[:, :128]
        grad_gu[1, at, :] = total[:, 128:]
        grad_d[:, at] = dot(all_hidden, block[:, at], TN).astype(BF)


def finish_kernel(own, other, result):
    core = lax.axis_index("dp") % 2
    result[:, half_at(core)] = own[...]
    result[:, half_at(1 - core)] = other[...]


def shape(dims, kind=BF):
    return jax.ShapeDtypeStruct(dims, kind)


def call(kernel, outs, flops, nbytes, specs, scratch=(), into=None, vmem=60):
    return pl.pallas_call(
        kernel,
        out_shape=outs,
        in_specs=specs,
        out_specs=jax.tree.map(lambda _: VMEM, outs) if into is None else into,
        scratch_shapes=scratch,
        cost_estimate=pl.CostEstimate(flops=flops, bytes_accessed=nbytes, transcendentals=0),
        compiler_params=pltpu.CompilerParams(vmem_limit_bytes=vmem << 20),
    )


def on_device(
    out_grad,
    route_probs,
    routes,
    replica_expert,
    saved_inputs,
    home_gate_up,
    home_down,
    replica_gate_up,
    replica_down,
):
    home_gu, home_d = home_gate_up[0], home_down[0]
    spare_gu, spare_d = replica_gate_up[0], replica_down[0]

    x_part = call(
        part_kernel,
        shape((32, 2, 2048)),
        10**3,
        10**5,
        [ANY],
        [pltpu.SemaphoreType.DMA(())],
    )(saved_inputs)
    x_part, routes, route_probs = lax.optimization_barrier((x_part, routes, route_probs))
    x_part = to_next(x_part)

    outgoing = call(
        prep_kernel,
        shape((1536, 256)),
        10**6,
        10**6,
        [VMEM] * 3,
        [pltpu.VMEM((1536, 256), BF), pltpu.SemaphoreType.DMA((4,))],
        ANY,
    )(routes.T, route_probs.T, out_grad)
    incoming = exchange(outgoing)

    saved, _ = lax.optimization_barrier((saved_inputs, outgoing))
    x = saved.reshape(256, 2048)
    acts, hidden, place = call(
        act_kernel,
        (shape((512, 128), F32), shape((256, 128)), shape((256, 16))),
        10**11,
        4 * 10**6,
        [VMEM] * 4,
    )(x, home_gu, spare_gu, routes.T)
    weights, _ = lax.optimization_barrier(((home_d, spare_d, home_gu, spare_gu), outgoing))
    packed = call(
        pack_kernel,
        shape((6144, 128)),
        10**6,
        10**6,
        [ANY] * 4,
        [pltpu.VMEM((6144, 128), BF), pltpu.SemaphoreType.DMA((21,))],
        ANY,
    )(*weights)
    packed = swap_cores(packed)
    acts_got = swap_cores(acts)
    incoming, acts, x_part, packed, acts_got = lax.optimization_barrier(
        (incoming, acts, x_part, packed, acts_got)
    )

    part, block_own = call(
        hidden_kernel,
        (shape((256, 256), F32), shape((384, 1024))),
        10**9,
        4 * 10**6,
        [ANY] * 4,
        [
            pltpu.VMEM((1536, 256), BF),
            pltpu.VMEM((2, 128, 1024), BF),
            pltpu.VMEM((2, 1024, 128), BF),
            pltpu.VMEM((256, 256), F32),
            pltpu.VMEM((384, 1024), BF),
            pltpu.SemaphoreType.DMA((5,)),
            pltpu.SemaphoreType.DMA((2,)),
        ],
        (ANY, ANY),
        vmem=50,
    )(incoming, home_d, spare_d, packed)
    pair, grads = call(
        rows_kernel,
        (pltpu.HBM((1024, 256), BF), pltpu.HBM((256, 256), BF)),
        10**9,
        4 * 10**6,
        [ANY] * 7,
        [
            pltpu.VMEM((2, 256, 256), F32),
            pltpu.VMEM((2, 512, 128), F32),
            pltpu.VMEM((2, 4, 1024, 128), BF),
            pltpu.VMEM((256, 256), BF),
            pltpu.VMEM((256, 1024), BF),
            pltpu.VMEM((1024, 256), BF),
            pltpu.SemaphoreType.DMA((12,)),
            pltpu.SemaphoreType.DMA((3,)),
        ],
        (HBM, HBM),
        vmem=50,
    )(part, swap_cores(part), acts, acts_got, home_gu, spare_gu, packed)
    returned = exchange(pair)

    x_part, incoming, _ = lax.optimization_barrier((x_part, incoming, pair))
    grad_gu, grad_d = call(
        weights_kernel,
        (shape((2, 2048, 128)), shape((128, 2048))),
        10**8,
        10**6,
        [SMEM] + [VMEM] * 9,
        [pltpu.VMEM((128, 2048), BF), pltpu.VMEM((384, 2048), BF)],
        vmem=40,
    )(
        replica_expert,
        x,
        x_part.reshape(64, 2048),
        swap_cores(x_part).reshape(64, 2048),
        block_own,
        swap_cores(incoming),
        grads,
        hidden,
        home_gu,
        home_d,
    )
    returned, grad_gu = lax.optimization_barrier((returned, grad_gu))

    mine, low = call(
        combine_kernel,
        (shape((16, 1024), F32), shape((16, 1024))),
        10**8,
        10**6,
        [VMEM] * 2,
        [pltpu.VMEM((256, 1024), BF)],
        vmem=28,
    )(returned, place)
    one = along_dp(low, lambda z: (z // 3 * 3 + (z + 1) % 3, 0))
    two = along_dp(low, lambda z: (z // 3 * 3 + (z + 2) % 3, 0))
    total = mine + one.astype(F32) + two.astype(F32)
    total = (total + along_dp(total.astype(BF), lambda z: ((z + 3) % 6, 0)).astype(F32)).astype(BF)
    input_grad = call(finish_kernel, shape((16, 2048)), 10**3, 10**5, [VMEM] * 2, vmem=28)(
        total, swap_cores(total)
    )
    return (input_grad, grad_gu[None], grad_d[None])


def solution(mesh):
    placed = (
        P("ep", None),
        P("ep", None),
        P("ep", None),
        P(),
        P("ep", None, None, None, None),
        P("ep", None, None, "dp"),
        P("ep", "dp", None),
        P("ep", None, None, "dp"),
        P("ep", "dp", None),
    )
    return jax.shard_map(
        on_device,
        mesh=mesh,
        in_specs=placed,
        out_specs=(P("ep", None), P("ep", None, None, "dp"), P("ep", "dp", None)),
        check_vma=False,
    )
```
